32 devices in a mesh: seq: 8 (over y, x, core), tensor: 4 (over z).
Axes of the slice: x: 2, y: 2, z: 4, core: 2. Of those that a mesh axis runs over, the one named last changes fastest.
Arguments:
- inputs: float32 [8192, 2048], P('seq', 'tensor'), may hold values from -6 to 6
- cotangent: float32 [8192, 2048], P('seq', 'tensor'), may hold values from -6 to 6
- proj_in: bfloat16 [2048, 6, 2048], P('seq', None, 'tensor'), may hold values from -0.125 to 0.125
- proj_out: bfloat16 [2048, 2, 2048], P('seq', None, 'tensor'), may hold values from -4 to 4
- ffn_in: bfloat16 [2048, 4, 5504], P('seq', None, 'tensor'), may hold values from -0.125 to 0.125
- ffn_down: bfloat16 [2048, 2, 5504], P('seq', None, 'tensor'), may hold values from -0.078125 to 0.078125
- gains: bfloat16 [2048, 5], P('seq'), may hold values from 0.5 to 1.5
Outputs:
- output: float32 [8192, 2048], P('seq', 'tensor')
- grad_inputs: float32 [8192, 2048], P('seq', 'tensor')
- grad_proj_in: float32 [2048, 6, 2048], P('seq', None, 'tensor')
- grad_proj_out: float32 [2048, 2, 2048], P('seq', None, 'tensor')
- grad_ffn_in: float32 [2048, 4, 5504], P('seq', None, 'tensor')
- grad_ffn_down: float32 [2048, 2, 5504], P('seq', None, 'tensor')
- grad_gains: float32 [2048, 5], P('seq')
The draws below stay inside these ranges and needn't reach their ends.
All inputs are finite; a program needn't handle non-finite values.
Results may differ from the reference program's by a relative error of at most 0.035.
Values may be sent and summed in bfloat16 or wider, within the bound.
A program may use at most 384 MiB of HBM per device.

```python
import jax
import jax.numpy as jnp
from jax import lax

D = 2048
HEADS = 16
HEAD_DIM = 128
FF = 5504
WINDOW = 1024
TOKENS = 8192


def block_scale(rng, shape, pieces, smallest, top_value):
    loudness = 1.0
    for axis_at, blocks in pieces:
        heights = jax.random.uniform(jax.random.fold_in(jax.random.fold_in(rng, 6), axis_at), (blocks,), jnp.float32, smallest / len(pieces), top_value / len(pieces))
        loudness = loudness * jnp.repeat(jnp.exp(heights), shape[axis_at] // blocks).reshape((-1,) + (1,) * (len(shape) - 1 - axis_at))
    return loudness


def bell_draw(own_key, shape, deviation, bound, split=(), kind=jnp.bfloat16):
    factor_of = block_scale(own_key, shape, split, -0.22, 0.18) if split else 1.0
    entries = jax.random.normal(own_key, shape, jnp.float32) * deviation * factor_of
    return jnp.minimum(jnp.maximum(entries, -bound), bound).astype(kind)


def setup_inputs(seed: int = 0) -> dict:
    seeds = jax.random.split(jax.random.key(seed), 8)
    return {
        "inputs": bell_draw(seeds[0], (TOKENS, D), 1.0, 6.0, ((0, 8), (1, 4)), jnp.float32),
        "cotangent": bell_draw(seeds[1], (TOKENS, D), 1.0, 6.0, ((0, 8), (1, 4)), jnp.float32),
        "proj_in": bell_draw(seeds[2], (D, 6, HEADS * HEAD_DIM), D ** -0.5, 0.125, ((0, 8), (2, 4))),
        "proj_out": bell_draw(seeds[3], (D, 2, HEADS * HEAD_DIM), (HEADS * HEAD_DIM // WINDOW) ** -0.5, 4.0, ((0, 8), (2, 4))),
        "ffn_in": bell_draw(seeds[4], (D, 4, FF), D ** -0.5, 0.125, ((0, 8), (2, 4))),
        "ffn_down": bell_draw(seeds[5], (D, 2, FF), FF ** -0.5, 0.078125, ((0, 8), (2, 4))),
        "gains": jnp.clip(1.0 + 0.1 * jax.random.normal(seeds[6], (D, 5), jnp.float32), 0.5, 1.5).astype(jnp.bfloat16),
    }


@jax.custom_vjp
def low(v):
    return lax.optimization_barrier(v.astype(jnp.bfloat16)).astype(jnp.float32)

@jax.custom_vjp
def low_back(v):
    return v

def low_keep(v):
    return (low(v), None)

def low_pass(kept, grad):
    return (grad,)

def back_keep(v):
    return (v, None)

def back_low(kept, grad):
    return (low(grad),)
low.defvjp(low_keep, low_pass)
low_back.defvjp(back_keep, back_low)
epsilon = 1e-06
floor_score = -1e+30
highest = lax.Precision.HIGHEST

def product(left, right):
    return jnp.dot(left, right, precision=highest)

def rms_scale(full_rows, gain_col):
    inverse = lax.rsqrt(lax.optimization_barrier(jnp.mean(full_rows * full_rows, axis=1, keepdims=True)) + epsilon)
    return low(full_rows * inverse * gain_col)

def attend(queries, key_rows, value_rows, query_pos, key_pos, horizon):
    scaling = HEAD_DIM ** (-0.5)
    scores = low_back(jnp.einsum('rhe,khe->hrk', queries, key_rows, precision=highest) * scaling)
    allowed_mask = ((key_pos[None, :] <= query_pos[:, None]) & (key_pos[None, :] > query_pos[:, None] - horizon) & (key_pos[None, :] >= 0))[None]
    masked = jnp.where(allowed_mask, scores, floor_score)
    highest_score = lax.optimization_barrier(jnp.max(masked, axis=2, keepdims=True))
    exponent = jnp.where(allowed_mask, jnp.exp(masked - highest_score), 0.0)
    probability = low(exponent / lax.optimization_barrier(jnp.sum(exponent, axis=2, keepdims=True)))
    return jnp.einsum('hrk,khe->rhe', probability, value_rows, precision=highest)

def window_attention(queries, key_rows, value_rows):
    extent = min(512, TOKENS)
    padding = jnp.zeros((WINDOW, HEADS, HEAD_DIM), jnp.float32)
    padded_keys = jnp.concatenate([padding, key_rows], axis=0)
    padded_values = jnp.concatenate([padding, value_rows], axis=0)

    def one_block(item):
        query_rows, anchor = item
        key_slice = lax.dynamic_slice_in_dim(padded_keys, anchor, WINDOW + extent, 0)
        value_slice = lax.dynamic_slice_in_dim(padded_values, anchor, WINDOW + extent, 0)
        query_pos = anchor + jnp.arange(extent, dtype=jnp.int32)
        key_pos = anchor - WINDOW + jnp.arange(WINDOW + extent, dtype=jnp.int32)
        return attend(query_rows, key_slice, value_slice, query_pos, key_pos, WINDOW)
    anchors = jnp.arange(TOKENS // extent, dtype=jnp.int32) * extent
    results = lax.map(jax.checkpoint(one_block), (queries.reshape(TOKENS // extent, extent, HEADS, HEAD_DIM), anchors))
    return results.reshape(TOKENS, HEADS * HEAD_DIM)

def cross_attention(queries, key_rows, value_rows):
    extent = min(256, TOKENS)
    key_pos = jnp.arange(TOKENS, dtype=jnp.int32)

    def one_block(item):
        query_rows, anchor = item
        query_pos = anchor + jnp.arange(extent, dtype=jnp.int32)
        return attend(query_rows, key_rows, value_rows, query_pos, key_pos, TOKENS + 1)
    anchors = jnp.arange(TOKENS // extent, dtype=jnp.int32) * extent
    results = lax.map(jax.checkpoint(one_block), (queries.reshape(TOKENS // extent, extent, HEADS, HEAD_DIM), anchors))
    return results.reshape(TOKENS, HEADS * HEAD_DIM)

def split_heads(rows):
    return rows.reshape(TOKENS, HEADS, HEAD_DIM)

def projected(normed, weight):
    return low_back(low(product(normed, weight)))

def feed(state, gain_col, weight_gate, weight_up, weight_down):
    normed = rms_scale(state, gain_col)
    gate = low_back(product(normed, weight_gate))
    upward = low_back(product(normed, weight_up))
    hidden = low(jax.nn.silu(gate) * upward)
    return low_back(product(hidden, weight_down.T))

def forward(inputs, proj_in, proj_out, ffn_in, ffn_down, gains):
    normed1 = rms_scale(inputs, gains[:, 0])
    query1 = projected(normed1, proj_in[:, 0])
    key1 = projected(normed1, proj_in[:, 1])
    value1 = projected(normed1, proj_in[:, 2])
    attended1 = low_back(low(window_attention(split_heads(query1), split_heads(key1), split_heads(value1))))
    state1 = inputs + low_back(product(attended1, proj_out[:, 0].T))
    state2 = state1 + feed(state1, gains[:, 1], ffn_in[:, 0], ffn_in[:, 1], ffn_down[:, 0])
    normed3 = rms_scale(state2, gains[:, 2])
    key2 = projected(normed3, proj_in[:, 3])
    value2 = projected(normed3, proj_in[:, 4])
    normed4 = rms_scale(state2, gains[:, 3])
    query2 = projected(normed4, proj_in[:, 5])
    attended2 = low_back(low(cross_attention(split_heads(query2), split_heads(key2), split_heads(value2))))
    state3 = state2 + low_back(product(attended2, proj_out[:, 1].T))
    return state3 + feed(state3, gains[:, 4], ffn_in[:, 2], ffn_in[:, 3], ffn_down[:, 1])

def reference(inputs, cotangent, proj_in, proj_out, ffn_in, ffn_down, gains):
    weights = [weight.astype(jnp.float32) for weight in (proj_in, proj_out, ffn_in, ffn_down, gains)]
    output, pullback = jax.vjp(forward, inputs, *weights)
    grads = pullback(cotangent)
    return (output, grads[0], grads[1], grads[2], grads[3], grads[4], grads[5])
```

```python
import functools

import jax
import jax.numpy as jnp
from jax import lax
from jax.experimental import pallas as pl
from jax.experimental.pallas import tpu as pltpu
from jax.sharding import PartitionSpec as P

HEAD_DIM = 128
WINDOW = 1024
SCALE = HEAD_DIM ** (-0.5)
SCALE2 = SCALE * 1.4426950408889634

epsilon = 1e-06
floor_score = -1e30
f32 = jnp.float32
bf16 = jnp.bfloat16
MIB = 1 << 20


def nt(left, right):
    return lax.dot_general(left, right, (((1,), (1,)), ((), ())), preferred_element_type=f32)


def tn(left, right):
    return lax.dot_general(left, right, (((0,), (0,)), ((), ())), preferred_element_type=f32)


def nn(left, right):
    return lax.dot_general(left, right, (((1,), (0,)), ((), ())), preferred_element_type=f32)


def row_dot(dout, out):
    product = dout.astype(f32) * out.astype(f32)
    return jnp.sum(product.T, axis=0, keepdims=True)


def near_allowed(span, size, start, rows):
    key = lax.broadcasted_iota(jnp.int32, (span, size), 0)
    query = lax.broadcasted_iota(jnp.int32, (span, size), 1)
    first = jnp.where(lax.axis_index("seq") == 0, rows - start, 0)
    return (key >= jnp.maximum(query + 1, first)) & (key <= query + WINDOW)


def near_forward_kernel(rows, q_ref, k_ref, v_ref, o_ref, stat_ref):
    size = q_ref.shape[0]
    span = WINDOW + size
    start = pl.multiple_of(pl.program_id(1) * size + (rows - WINDOW), size)
    allowed = near_allowed(span, size, start, rows)
    scores = nt(k_ref[pl.ds(start, span), :], q_ref[...]) * SCALE2
    scores = jnp.where(allowed, scores, floor_score)
    top = jnp.max(scores, axis=0, keepdims=True)
    weight = jnp.exp2(scores - top)
    total = jnp.sum(weight, axis=0, keepdims=True)
    mixed = tn(v_ref[pl.ds(start, span), :], weight.astype(bf16)) / total
    o_ref[...] = mixed.T.astype(bf16)
    stat_ref[0] = top + jnp.log2(total)


def near_forward(queries, keys, values):
    rows, width = queries.shape
    heads, size = width // HEAD_DIM, min(256, rows)
    own = pl.BlockSpec((size, HEAD_DIM), lambda h, b: (b, h))
    span = pl.BlockSpec((keys.shape[0], HEAD_DIM), lambda h, b: (0, h))
    stat = pl.BlockSpec((1, 1, size), lambda h, b: (h, 0, b))
    pairs = heads * rows * (WINDOW + size)
    return pl.pallas_call(
        functools.partial(near_forward_kernel, rows),
        grid=(heads, rows // size),
        in_specs=[own, span, span],
        out_specs=[own, stat],
        out_shape=[
            jax.ShapeDtypeStruct((rows, width), bf16),
            jax.ShapeDtypeStruct((heads, 1, rows), f32),
        ],
        compiler_params=pltpu.CompilerParams(vmem_limit_bytes=40 * MIB),
        cost_estimate=pl.CostEstimate(
            flops=pairs * 4 * HEAD_DIM * 2, bytes_accessed=rows * width * 12, transcendentals=pairs
        ),
        name="near_forward",
    )(queries, keys, values)


def near_backward_kernel(rows, q_ref, k_ref, v_ref, do_ref, o_ref, stat_ref, dq_ref, dk_ref, dv_ref):
    size = q_ref.shape[0]
    span = WINDOW + size
    start = pl.multiple_of(pl.program_id(1) * size + (rows - WINDOW), size)

    @pl.when(pl.program_id(1) == 0)
    def clear():
        dk_ref[...] = jnp.zeros_like(dk_ref)
        dv_ref[...] = jnp.zeros_like(dv_ref)

    place = pl.ds(start, span)
    queries, dout = q_ref[...], do_ref[...]
    keys, values = k_ref[place, :], v_ref[place, :]
    inner = row_dot(dout, o_ref[...])
    allowed = near_allowed(span, size, start, rows)
    scores = nt(keys, queries) * SCALE2 - stat_ref[0]
    weight = jnp.exp2(jnp.where(allowed, scores, floor_score))
    dscore = (weight * (nt(values, dout) - inner)).astype(bf16)
    dv_ref[place, :] += nn(weight.astype(bf16), dout)
    dk_ref[place, :] += nn(dscore, queries) * SCALE
    dq_ref[...] = (tn(keys, dscore) * SCALE).T.astype(bf16)


def near_backward(queries, keys, values, dresult, result, stats):
    rows, width = queries.shape
    heads, size = width // HEAD_DIM, min(256, rows)
    own = pl.BlockSpec((size, HEAD_DIM), lambda h, b: (b, h))
    span = pl.BlockSpec((keys.shape[0], HEAD_DIM), lambda h, b: (0, h))
    stat = pl.BlockSpec((1, 1, size), lambda h, b: (h, 0, b))
    pairs = heads * rows * (WINDOW + size)
    return pl.pallas_call(
        functools.partial(near_backward_kernel, rows),
        grid=(heads, rows // size),
        in_specs=[own, span, span, own, own, stat],
        out_specs=[own, span, span],
        out_shape=[
            jax.ShapeDtypeStruct((rows, width), bf16),
            jax.ShapeDtypeStruct(keys.shape, f32),
            jax.ShapeDtypeStruct(keys.shape, f32),
        ],
        compiler_params=pltpu.CompilerParams(vmem_limit_bytes=40 * MIB),
        cost_estimate=pl.CostEstimate(
            flops=pairs * 10 * HEAD_DIM * 2, bytes_accessed=rows * width * 32, transcendentals=pairs
        ),
        name="near_backward",
    )(queries, keys, values, dresult, result, stats)


def far_place(block):
    mine, count = lax.axis_index("seq"), lax.axis_size("seq")
    return jnp.where(block == 0, 2 * mine, 2 * count - 1 - 2 * mine)


def triangle(size, start, width):
    key = lax.broadcasted_iota(jnp.int32, (size, width), 0)
    query = lax.broadcasted_iota(jnp.int32, (size, width), 1)
    return key <= query + start


def query_parts(size):
    return [(start, size // 2) for start in (0, size // 2)]


def far_forward_kernel(q_ref, kv_ref, o_ref, stat_ref, top_ref, sum_ref, acc_ref):
    size = q_ref.shape[0]
    last = far_place(pl.program_id(1))
    top_ref[...] = jnp.full_like(top_ref, floor_score)
    sum_ref[...] = jnp.zeros_like(sum_ref)
    acc_ref[...] = jnp.zeros_like(acc_ref)

    def step(index, masked):
        place = pl.ds(pl.multiple_of(index * size, size), size)
        keys, values = kv_ref[place, :HEAD_DIM], kv_ref[place, HEAD_DIM:]
        parts = query_parts(size)
        all_scores = [nt(keys, q_ref[start : start + width, :]) for start, width in parts]
        for (start, width), scores in zip(parts, all_scores):
            own = slice(start, start + width)
            scores = scores * SCALE2
            if masked:
                scores = jnp.where(triangle(size, start, width), scores, floor_score)
            before = top_ref[:, own]
            top = jnp.maximum(before, jnp.max(scores, axis=0, keepdims=True))
            weight = jnp.exp2(scores - top)
            fade = jnp.exp2(before - top)
            top_ref[:, own] = top
            sum_ref[:, own] = sum_ref[:, own] * fade + jnp.sum(weight, axis=0, keepdims=True)
            acc_ref[:, own] = acc_ref[:, own] * fade + tn(values, weight.astype(bf16))

    @pl.loop(0, last)
    def earlier(index):
        step(index, False)

    step(last, True)
    o_ref[...] = (acc_ref[...] / sum_ref[...]).T.astype(bf16)
    stat_ref[0] = top_ref[...] + jnp.log2(sum_ref[...])


def far_forward(queries, pairs_kv):
    rows, width = queries.shape
    heads, size = width // HEAD_DIM, rows // 2
    own = pl.BlockSpec((size, HEAD_DIM), lambda h, b: (b, h))
    whole = pl.BlockSpec((pairs_kv.shape[0], 2 * HEAD_DIM), lambda h, b: (0, h))
    stat = pl.BlockSpec((1, 1, size), lambda h, b: (h, 0, b))
    pairs = heads * rows * pairs_kv.shape[0] // 2
    return pl.pallas_call(
        far_forward_kernel,
        grid=(heads, 2),
        in_specs=[own, whole],
        out_specs=[own, stat],
        out_shape=[
            jax.ShapeDtypeStruct((rows, width), bf16),
            jax.ShapeDtypeStruct((heads, 1, rows), f32),
        ],
        scratch_shapes=[
            pltpu.VMEM((1, size), f32),
            pltpu.VMEM((1, size), f32),
            pltpu.VMEM((HEAD_DIM, size), f32),
        ],
        compiler_params=pltpu.CompilerParams(vmem_limit_bytes=48 * MIB),
        cost_estimate=pl.CostEstimate(
            flops=pairs * 4 * HEAD_DIM * 2,
            bytes_accessed=pairs_kv.shape[0] * width * 4,
            transcendentals=pairs,
        ),
        name="far_forward",
    )(queries, pairs_kv)


def far_backward_kernel(
    q_ref, kv_ref, do_ref, o_ref, stat_ref, dq_ref, dkv_ref, dq_acc, dk_acc, dv_acc
):
    size = q_ref.shape[0]
    block = pl.program_id(1)
    last = far_place(block)

    @pl.when(block == 0)
    def clear():
        dk_acc[...] = jnp.zeros_like(dk_acc)
        dv_acc[...] = jnp.zeros_like(dv_acc)

    dq_acc[...] = jnp.zeros_like(dq_acc)
    inner = row_dot(do_ref[...], o_ref[...])

    def step(index, masked):
        place = pl.ds(pl.multiple_of(index * size, size), size)
        keys, values = kv_ref[place, :HEAD_DIM], kv_ref[place, HEAD_DIM:]
        parts = []
        for start, width in query_parts(size):
            own = slice(start, start + width)
            queries, dout = q_ref[own, :], do_ref[own, :]
            parts.append((start, width, own, queries, dout, nt(keys, queries), nt(values, dout)))
        dvalues, dkeys = [], []
        for start, width, own, queries, dout, scores, dweight in parts:
            scores = scores * SCALE2 - stat_ref[0, :, own]
            if masked:
                scores = jnp.where(triangle(size, start, width), scores, floor_score)
            weight = jnp.exp2(scores)
            dscore = (weight * (dweight - inner[:, own])).astype(bf16)
            dvalues.append(nn(weight.astype(bf16), dout))
            dkeys.append(nn(dscore, queries))
            dq_acc[:, own] += tn(keys, dscore)
        dv_acc[place, :] += dvalues[0] + dvalues[1]
        dk_acc[place, :] += dkeys[0] + dkeys[1]

    @pl.loop(0, last)
    def earlier(index):
        step(index, False)

    step(last, True)
    dq_ref[...] = (dq_acc[...] * SCALE).T.astype(bf16)

    @pl.when(block == 1)
    def leave():
        dkv_ref[:, :HEAD_DIM] = (dk_acc[...] * SCALE).astype(bf16)
        dkv_ref[:, HEAD_DIM:] = dv_acc[...].astype(bf16)


def far_backward(queries, pairs_kv, dresult, result, stats):
    rows, width = queries.shape
    heads, size = width // HEAD_DIM, rows // 2
    tokens = pairs_kv.shape[0]
    own = pl.BlockSpec((size, HEAD_DIM), lambda h, b: (b, h))
    whole = pl.BlockSpec((tokens, 2 * HEAD_DIM), lambda h, b: (0, h))
    stat = pl.BlockSpec((1, 1, size), lambda h, b: (h, 0, b))
    pairs = heads * rows * tokens // 2
    return pl.pallas_call(
        far_backward_kernel,
        grid=(heads, 2),
        in_specs=[own, whole, own, own, stat],
        out_specs=[own, whole],
        out_shape=[
            jax.ShapeDtypeStruct((rows, width), bf16),
            jax.ShapeDtypeStruct(pairs_kv.shape, bf16),
        ],
        scratch_shapes=[
            pltpu.VMEM((HEAD_DIM, size), f32),
            pltpu.VMEM((tokens, HEAD_DIM), f32),
            pltpu.VMEM((tokens, HEAD_DIM), f32),
        ],
        compiler_params=pltpu.CompilerParams(vmem_limit_bytes=60 * MIB),
        cost_estimate=pl.CostEstimate(
            flops=pairs * 10 * HEAD_DIM * 2,
            bytes_accessed=tokens * width * 8,
            transcendentals=pairs,
        ),
        name="far_backward",
    )(queries, pairs_kv, dresult, result, stats)


def greet_neighbours(mine, count, partner=None):
    barrier = pltpu.get_barrier_semaphore()
    sides = ((-1, mine > 0), (1, mine < count - 1))
    if partner is not None:
        pl.semaphore_signal(
            barrier, inc=1, device_id={"seq": partner}, device_id_type=pl.DeviceIdType.MESH
        )
    for side, present in sides:

        @pl.when(present)
        def greet():
            pl.semaphore_signal(
                barrier,
                inc=1,
                device_id={"tensor": mine + side},
                device_id_type=pl.DeviceIdType.MESH,
            )

    others = 0 if partner is None else 1
    pl.semaphore_wait(barrier, others + sum(present.astype(jnp.int32) for _, present in sides))


def chain_kernel(chunk, turns, own_only, part_ref, base_ref, *refs):
    if own_only:
        own_ref, out_ref, *refs = refs
    else:
        out_ref, *refs = refs
    sum_ref, rs_send, rs_recv, ag_send, ag_recv, *refs = refs
    turn = refs[0] if turns else None
    count = lax.axis_size("tensor")
    mine = lax.axis_index("tensor")
    rows, depth = part_ref.shape
    half, pieces, slack = depth // 2, rows // chunk, 2
    hops = count // 2 - 1 if own_only else count - 1
    ticks = pieces + slack * (count - 1 + hops)
    core = lax.rem(lax.axis_index("seq"), 2)
    partner = lax.axis_index("seq") + 1 - 2 * core if turns else None
    greet_neighbours(mine, count, partner)
    if turns:

        @pl.when(core == 1)
        def follow():
            pl.semaphore_wait(turn, 1)

    flows = [(0, mine, -1), (1, count - 1 - mine, 1)]

    def area(flow, piece):
        return (pl.ds(pl.multiple_of(piece * chunk, chunk), chunk), pl.ds(flow * half, half))

    def inward(flow, step, piece, source):
        rows_cols = area(flow, piece)
        return pltpu.make_async_remote_copy(
            src_ref=source.at[rows_cols],
            dst_ref=sum_ref.at[rows_cols],
            send_sem=rs_send.at[flow, piece],
            recv_sem=rs_recv.at[flow, piece],
            device_id={"tensor": mine + step},
            device_id_type=pl.DeviceIdType.MESH,
        )

    def outward(flow, step, piece, hop):
        rows_cols = area(flow, piece)
        if own_only:
            width = depth // count
            start, length = (hop + 1) * width, half - (hop + 1) * width
            rows_cols = (rows_cols[0], pl.ds(half if flow else start, length))
        return pltpu.make_async_remote_copy(
            src_ref=out_ref.at[rows_cols],
            dst_ref=out_ref.at[rows_cols],
            send_sem=ag_send.at[flow, piece],
            recv_sem=ag_recv.at[flow, piece],
            device_id={"tensor": mine - step},
            device_id_type=pl.DeviceIdType.MESH,
        )

    @pl.loop(0, ticks)
    def beat(tick):
        if turns:

            @pl.when((core == 0) & (tick == ticks * 7 // 8))
            def lead():
                pl.semaphore_signal(
                    turn, inc=1, device_id={"seq": partner}, device_id_type=pl.DeviceIdType.MESH
                )

        for flow, far, step in flows:
            piece = tick - slack * (count - 1 - far)
            live = (piece >= 0) & (piece < pieces)

            @pl.when(live & (far == count - 1))
            def leaf():
                inward(flow, step, piece, part_ref).start()

            @pl.when(live & (far < count - 1))
            def arrived():
                inward(flow, step, piece, sum_ref).wait_recv()

            @pl.when(live & (far < count - 1) & (far > 0))
            def middle():
                rows_cols = area(flow, piece)
                sum_ref[rows_cols] = (
                    sum_ref[rows_cols].astype(f32) + part_ref[rows_cols].astype(f32)
                ).astype(bf16)
                inward(flow, step, piece, sum_ref).start()

            @pl.when(live & (far == 0))
            def root():
                rows_cols = area(flow, piece)
                out_ref[rows_cols] = (
                    sum_ref[rows_cols].astype(f32)
                    + part_ref[rows_cols].astype(f32)
                    + base_ref[rows_cols].astype(f32)
                ).astype(bf16)
                if hops > 0:
                    outward(flow, step, piece, 0).start()

        for flow, far, step in flows:
            piece = tick - slack * (count - 1 + far)
            live = (piece >= 0) & (piece < pieces)
            for hop in range(hops) if own_only else (0,):

                @pl.when(live & ((far == hop + 1) if own_only else (far > 0)))
                def landed():
                    outward(flow, step, piece, hop).wait_recv()

                if own_only and hop + 1 == hops:
                    continue

                @pl.when(live & ((far == hop + 1) if own_only else (far > 0) & (far < hops)))
                def forward():
                    outward(flow, step, piece, hop + 1).start()

    if own_only:
        width = depth // count
        own_ref[...] = out_ref[:, pl.ds(pl.multiple_of(mine * width, width), width)].astype(f32)

    @pl.loop(0, pieces)
    def finish(piece):
        for flow, far, step in flows:

            @pl.when(far > 0)
            def sent_in():
                inward(flow, step, piece, sum_ref).wait_send()

            for hop in range(hops) if own_only else (0,):

                @pl.when((far == hop) if own_only else (far < hops))
                def sent_out():
                    outward(flow, step, piece, hop).wait_send()


def chain_sum(partial_value, base, turns=0, own_only=False):
    turns = turns if lax.axis_size("seq") % 2 == 0 else 0
    rows, depth = base.shape
    chunk = 32
    pieces = rows // chunk
    own_width = depth // lax.axis_size("tensor") if own_only else depth
    whole = pl.BlockSpec(memory_space=pltpu.VMEM)
    return pl.pallas_call(
        functools.partial(chain_kernel, chunk, turns, own_only),
        in_specs=[whole, whole],
        out_specs=whole,
        out_shape=jax.ShapeDtypeStruct((rows, own_width), f32 if own_only else bf16),
        scratch_shapes=[pltpu.VMEM((rows, depth), bf16)] * (2 if own_only else 1)
        + [pltpu.SemaphoreType.DMA((2, pieces))] * 4
        + [pltpu.SemaphoreType.REGULAR] * (turns > 0),
        compiler_params=pltpu.CompilerParams(
            collective_id=1 + turns if turns else 6 * own_only, has_side_effects=True, vmem_limit_bytes=32 * MIB
        ),
        cost_estimate=pl.CostEstimate(
            flops=10**11, bytes_accessed=rows * depth * 6, transcendentals=0
        ),
        name="chain_sum_turns" if turns else "chain_own" if own_only else "chain_sum",
    )(partial_value.astype(bf16), base)


def spread_kernel(chunk, own_ref, out_ref, send_sem, recv_sem):
    count = lax.axis_size("tensor")
    mine = lax.axis_index("tensor")
    rows, width = own_ref.shape
    pieces = rows // chunk
    greet_neighbours(mine, count)

    def copy(way, side, hop, piece):
        source = jnp.clip(mine - side * hop, 0, count - 1)
        place = (
            pl.ds(pl.multiple_of(piece * chunk, chunk), chunk),
            pl.ds(pl.multiple_of(source * width, width), width),
        )
        return pltpu.make_async_remote_copy(
            src_ref=out_ref.at[place],
            dst_ref=out_ref.at[place],
            send_sem=send_sem.at[way, hop, piece],
            recv_sem=recv_sem.at[way, hop, piece],
            device_id={"tensor": jnp.clip(mine + side, 0, count - 1)},
            device_id_type=pl.DeviceIdType.MESH,
        )

    def landing(way, side, hop, piece):
        source = jnp.clip(mine - side * hop, 0, count - 1)
        place = (
            pl.ds(pl.multiple_of(piece * chunk, chunk), chunk),
            pl.ds(pl.multiple_of(source * width, width), width),
        )
        return pltpu.make_async_remote_copy(
            src_ref=out_ref.at[place],
            dst_ref=out_ref.at[place],
            send_sem=send_sem.at[way, hop - 1, piece],
            recv_sem=recv_sem.at[way, hop - 1, piece],
            device_id={"tensor": jnp.clip(mine + side, 0, count - 1)},
            device_id_type=pl.DeviceIdType.MESH,
        )

    ways = [(0, 1), (1, -1)]
    out_ref[:, pl.ds(pl.multiple_of(mine * width, width), width)] = own_ref[...].astype(bf16)

    for hop in range(count):

        @pl.loop(0, pieces)
        def pass_on(piece):
            for way, side in ways:
                source, target = mine - side * hop, mine + side
                held = (source >= 0) & (source < count)

                if hop > 0:

                    @pl.when(held)
                    def landed():
                        landing(way, side, hop, piece).wait_recv()

                if hop < count - 1:

                    @pl.when(held & (target >= 0) & (target < count))
                    def forward():
                        copy(way, side, hop, piece).start()

    for hop in range(count - 1):

        @pl.loop(0, pieces)
        def finish(piece):
            for way, side in ways:
                source, target = mine - side * hop, mine + side

                @pl.when((source >= 0) & (source < count) & (target >= 0) & (target < count))
                def sent():
                    copy(way, side, hop, piece).wait_send()


def spread(own_rows):
    rows, width = own_rows.shape
    count, chunk = lax.axis_size("tensor"), 128
    whole = pl.BlockSpec(memory_space=pltpu.VMEM)
    return pl.pallas_call(
        functools.partial(spread_kernel, chunk),
        in_specs=[whole],
        out_specs=whole,
        out_shape=jax.ShapeDtypeStruct((rows, width * count), bf16),
        scratch_shapes=[pltpu.SemaphoreType.DMA((2, count - 1, rows // chunk))] * 2,
        compiler_params=pltpu.CompilerParams(
            collective_id=1, has_side_effects=True, vmem_limit_bytes=24 * MIB
        ),
        cost_estimate=pl.CostEstimate(
            flops=7 * 10**10, bytes_accessed=rows * width * 20, transcendentals=0
        ),
        name="spread",
    )(own_rows)


def small_kernel(own_ref, out_ref, land_ref, send_sem, recv_sem):
    count = lax.axis_size("tensor")
    mine = lax.axis_index("tensor")
    barrier = pltpu.get_barrier_semaphore()
    others = [lax.rem(mine + step, count) for step in range(1, count)]
    for other in others:
        pl.semaphore_signal(
            barrier, inc=1, device_id={"tensor": other}, device_id_type=pl.DeviceIdType.MESH
        )
    pl.semaphore_wait(barrier, count - 1)
    copies = [
        pltpu.make_async_remote_copy(
            src_ref=own_ref,
            dst_ref=land_ref.at[mine],
            send_sem=send_sem.at[slot],
            recv_sem=recv_sem.at[slot],
            device_id={"tensor": other},
            device_id_type=pl.DeviceIdType.MESH,
        )
        for slot, other in enumerate(others)
    ]
    for copy in copies:
        copy.start()
    land_ref[mine] = own_ref[...]
    for copy in copies:
        copy.wait()
    total = land_ref[0]
    for place in range(1, count):
        total = total + land_ref[place]
    out_ref[...] = total


def small_sum(value):
    count = lax.axis_size("tensor")
    whole = pl.BlockSpec(memory_space=pltpu.VMEM)
    return pl.pallas_call(
        small_kernel,
        in_specs=[whole],
        out_specs=whole,
        out_shape=jax.ShapeDtypeStruct(value.shape, f32),
        scratch_shapes=[pltpu.VMEM((count, *value.shape), f32)]
        + [pltpu.SemaphoreType.DMA((count - 1,))] * 2,
        compiler_params=pltpu.CompilerParams(collective_id=5, has_side_effects=True),
        cost_estimate=pl.CostEstimate(flops=10**9, bytes_accessed=value.size * 8, transcendentals=0),
        name="small_sum",
    )(value)


def shifted(block, axis, distance):
    devices = range(lax.axis_size(axis))
    route = [(i - distance, i) for i in devices if i - distance in devices]
    return lax.ppermute(block, axis, route)


def swapped(block):
    count, half = lax.axis_size("seq"), block.shape[0] // 2
    other = lax.ppermute(block[half:], "seq", [(i, count - 1 - i) for i in range(count)])
    return jnp.concatenate([block[:half], other], axis=0)


def gathered(weight):
    return lax.all_gather(weight, "seq", axis=0, tiled=True)


def scattered(grad):
    return lax.psum_scatter(grad.astype(bf16), "seq", scatter_dimension=0, tiled=True)


def together(value, grads):
    return lax.optimization_barrier((value.astype(bf16), tuple(g.astype(bf16) for g in grads)))


def inverse_rms(rows):
    return lax.rsqrt(jnp.mean(rows * rows, axis=1, keepdims=True) + epsilon)


def norm_back(rows, gain_row, gradient):
    inverse = inverse_rms(rows)
    scaled = gradient * gain_row
    cubed = inverse * inverse * inverse
    dfull = inverse * scaled - rows * cubed * jnp.mean(scaled * rows, axis=1, keepdims=True)
    return (dfull, jnp.sum(gradient * rows * inverse, axis=0, keepdims=True))


def row_block(size, width):
    return pl.BlockSpec((size, width), lambda i: (i, 0))


def resident(array):
    return pl.BlockSpec(array.shape, lambda i: (0, 0), pipeline_mode=pl.Buffered(1))


def blocks_call(kernel, name, rows, size, ins, outs, flops, weights=()):
    in_specs = [row_block(size, x.shape[1]) if cut else resident(x) for x, cut in ins]
    in_specs += [pl.BlockSpec(memory_space=pl.ANY) for _ in weights]
    scratch = [pltpu.VMEM(x.shape, x.dtype) for x in weights]
    if weights:
        scratch.append(pltpu.SemaphoreType.DMA((3,)))
    out_specs = [
        row_block(size, shape[1]) if cut else pl.BlockSpec(shape, lambda i: (0, 0))
        for shape, _, cut in outs
    ]
    return pl.pallas_call(
        kernel,
        grid=(rows // size,),
        in_specs=in_specs,
        out_specs=out_specs,
        out_shape=[jax.ShapeDtypeStruct(shape, kind) for shape, kind, _ in outs],
        compiler_params=pltpu.CompilerParams(vmem_limit_bytes=56 * MIB),
        cost_estimate=pl.CostEstimate(
            flops=flops, bytes_accessed=sum(x.size * 2 for x, _ in ins), transcendentals=0
        ),
        scratch_shapes=scratch,
        name=name,
    )(*[x for x, _ in ins], *weights)


def project_kernel(parts, full_ref, weight_ref, *refs):
    gains, outs = refs[: len(parts)], refs[len(parts) :]
    rows = full_ref[...].astype(f32)
    scaled = rows * inverse_rms(rows)
    for place, (start, width) in enumerate(parts):
        normed = (scaled * gains[place][...]).astype(bf16)
        outs[2 * place][...] = normed
        outs[2 * place + 1][...] = nn(normed, weight_ref[:, start : start + width]).astype(bf16)


def project(full, weight, parts):
    rows, depth = full.shape
    outs = []
    for _, _, width in parts:
        outs += [((rows, depth), bf16, True), ((rows, width), bf16, True)]
    return blocks_call(
        functools.partial(project_kernel, [part[1:] for part in parts]),
        "project",
        rows,
        min(256, rows),
        [(full, True), (weight, False)] + [(gain, False) for gain, _, _ in parts],
        outs,
        2 * rows * depth * sum(width for _, _, width in parts),
    )


def project_back_kernel(parts, full_ref, weight_ref, *refs):
    count = len(parts)
    gains, grads, dfull_ref, dgains = refs[:count], refs[count : 2 * count], refs[2 * count], refs[2 * count + 1 :]

    @pl.when(pl.program_id(0) == 0)
    def clear():
        for ref in dgains:
            ref[...] = jnp.zeros_like(ref)

    rows = full_ref[...].astype(f32)
    total = jnp.zeros_like(rows)
    for place, (start, width) in enumerate(parts):
        dnormed = nt(grads[place][...], weight_ref[:, start : start + width])
        dfull, dgain = norm_back(rows, gains[place][...], dnormed)
        total = total + dfull
        dgains[place][...] += dgain
    dfull_ref[...] = total.astype(bf16)


def project_back(full, weight, parts):
    rows, depth = full.shape
    return blocks_call(
        functools.partial(project_back_kernel, [part[1:3] for part in parts]),
        "project_back",
        rows,
        min(256, rows),
        [(full, True), (weight, False)]
        + [(part[0], False) for part in parts]
        + [(part[3], True) for part in parts],
        [((rows, depth), bf16, True)] + [((1, depth), f32, False)] * len(parts),
        2 * rows * depth * sum(part[2] for part in parts),
    )


def weight_copies(pair_hbm, down_hbm, pair_weight, down_weight, sems):
    half = down_weight.shape[1]
    gate, upward = pl.ds(0, half), pl.ds(half, half)
    return [
        pltpu.make_async_copy(pair_hbm.at[:, gate], pair_weight.at[:, gate], sems.at[0]),
        pltpu.make_async_copy(pair_hbm.at[:, upward], pair_weight.at[:, upward], sems.at[1]),
        pltpu.make_async_copy(down_hbm, down_weight, sems.at[2]),
    ]


def at_first(action):
    pl.when(pl.program_id(0) == 0)(action)


def feed_forward_kernel(
    full_ref, gain_ref, pair_hbm, down_hbm, branch_ref, normed_ref, pair_ref, hidden_ref, *weights
):
    pair_weight, down_weight, sems = weights
    copies = weight_copies(pair_hbm, down_hbm, pair_weight, down_weight, sems)
    half = hidden_ref.shape[1]

    @at_first
    def fetch():
        for copy in copies:
            copy.start()

    rows = full_ref[...].astype(f32)
    normed = (rows * inverse_rms(rows) * gain_ref[...]).astype(bf16)
    normed_ref[...] = normed
    at_first(copies[0].wait)
    gate = nn(normed, pair_weight[:, :half])
    at_first(copies[1].wait)
    upward = nn(normed, pair_weight[:, half:])
    pair_ref[:, :half] = gate.astype(bf16)
    pair_ref[:, half:] = upward.astype(bf16)
    hidden = (gate * jax.nn.sigmoid(gate) * upward).astype(bf16)
    hidden_ref[...] = hidden
    at_first(copies[2].wait)
    branch_ref[...] = nt(hidden, down_weight[...]).astype(bf16)


def feed_forward(full, gain, weight_pair, weight_down):
    rows, depth = full.shape
    half = weight_down.shape[1]
    branch, normed, pair, hidden = blocks_call(
        feed_forward_kernel,
        "feed_forward",
        rows,
        min(512, rows),
        [(full, True), (gain, False)],
        [
            ((rows, depth), bf16, True),
            ((rows, depth), bf16, True),
            ((rows, 2 * half), bf16, True),
            ((rows, half), bf16, True),
        ],
        6 * rows * depth * half,
        (weight_pair, weight_down),
    )
    return (branch, (full, normed, pair, hidden))


def feed_backward_kernel(
    dout_ref, full_ref, pair_ref, gain_ref, pair_hbm, down_hbm, dfull_ref, dpair_ref, dgain_ref, *weights
):
    pair_weight, down_weight, sems = weights
    copies = weight_copies(pair_hbm, down_hbm, pair_weight, down_weight, sems)
    half = down_weight.shape[1]

    @at_first
    def fetch():
        for copy in copies[::-1]:
            copy.start()
        dgain_ref[...] = jnp.zeros_like(dgain_ref)
        copies[2].wait()

    dhidden = nn(dout_ref[...], down_weight[...])
    gate, upward = pair_ref[:, :half].astype(f32), pair_ref[:, half:].astype(f32)
    sigma = jax.nn.sigmoid(gate)
    dpair_ref[:, :half] = (dhidden * upward * sigma * (1.0 + gate * (1.0 - sigma))).astype(bf16)
    dpair_ref[:, half:] = (dhidden * gate * sigma).astype(bf16)

    @at_first
    def have_pair():
        copies[0].wait()
        copies[1].wait()

    dfull, dgain = norm_back(
        full_ref[...].astype(f32), gain_ref[...], nt(dpair_ref[...], pair_weight[...])
    )
    dfull_ref[...] = dfull.astype(bf16)
    dgain_ref[...] += dgain


def feed_backward(dbranch, gain, weight_pair, weight_down, saved):
    full, normed, pair, hidden = saved
    rows, depth = full.shape
    half = weight_down.shape[1]
    dfull, dpair, grad_gain = blocks_call(
        feed_backward_kernel,
        "feed_backward",
        rows,
        min(512, rows),
        [
            (dbranch, True),
            (full, True),
            (pair, True),
            (gain, False),
        ],
        [((rows, depth), bf16, True), ((rows, 2 * half), bf16, True), ((1, depth), f32, False)],
        6 * rows * depth * half,
        (weight_pair, weight_down),
    )
    return (dfull, [(normed, dpair), (dbranch, hidden)], grad_gain)


def gradients_kernel(count, *refs):
    lefts, rights, extra, out_ref = refs[:count], refs[count : 2 * count], refs[2 * count : -1], refs[-1]
    start = 0
    for left, right in zip(lefts, rights):
        width = right.shape[1]
        out_ref[:, start : start + width] = tn(left[...], right[...]).astype(bf16)
        start += width
    for ref in extra:
        out_ref[:, start : start + ref.shape[1]] = ref[...]
        start += ref.shape[1]


def gradients(pairs, extra=()):
    rows, depth = pairs[0][0].shape
    size = min(512, depth)
    total = sum(right.shape[1] for _, right in pairs) + sum(x.shape[1] for x in extra)
    return pl.pallas_call(
        functools.partial(gradients_kernel, len(pairs)),
        grid=(depth // size,),
        in_specs=[pl.BlockSpec((rows, size), lambda i: (0, i)) for _ in pairs]
        + [resident(right) for _, right in pairs]
        + [row_block(size, x.shape[1]) for x in extra],
        out_specs=row_block(size, total),
        out_shape=jax.ShapeDtypeStruct((depth, total), bf16),
        compiler_params=pltpu.CompilerParams(vmem_limit_bytes=56 * MIB),
        cost_estimate=pl.CostEstimate(
            flops=2 * rows * depth * total, bytes_accessed=depth * total * 4, transcendentals=0
        ),
        name="gradients",
    )(*[left for left, _ in pairs], *[right for _, right in pairs], *extra)


def padded(width):
    return -(-width // 128) * 128


def pad_columns(weight):
    width = weight.shape[1]
    return jnp.pad(weight, ((0, 0), (0, padded(width) - width)))


def shards(inputs, cotangent, proj_in, proj_out, ffn_in, ffn_down, gains):
    rows = inputs.shape[0]
    width = proj_in.shape[2]
    depth = proj_in.shape[0]
    heads = width // HEAD_DIM
    hidden_width = ffn_down.shape[2]
    half = padded(hidden_width)
    packed = gathered(
        jnp.concatenate([proj_in[:, 0:3].reshape(depth, 3 * width), pad_columns(gains)], axis=1)
    )
    gain_rows = nt(jnp.eye(8, 5, dtype=bf16), packed[:, 3 * width : 3 * width + 5])
    gain = [gain_rows[j : j + 1] for j in range(5)]
    full0 = spread(inputs)
    w_out1 = gathered(proj_out[:, 0])
    own_pair1 = jnp.concatenate([pad_columns(ffn_in[:, j]) for j in (0, 1)], axis=1)
    own_pair2 = jnp.concatenate([pad_columns(ffn_in[:, j]) for j in (2, 3)], axis=1)
    cache_in = proj_in[:, 3:5].reshape(depth, 2, heads, HEAD_DIM).transpose(0, 2, 1, 3)
    own_cross = jnp.concatenate([cache_in.reshape(depth, 2 * width), proj_in[:, 5]], axis=1)

    normed1, own = project(full0, packed, [(gain[0], 0, 3 * width)])
    query1 = own[:, :width]
    earlier = shifted(own[:, width:], "seq", 1)
    earlier, own_pair1, own_down1 = lax.optimization_barrier(
        (earlier, own_pair1, ffn_down[:, 0])
    )
    w_pair1 = gathered(own_pair1)
    w_down1 = gathered(pad_columns(own_down1))
    w_cross = gathered(own_cross)
    w_out2 = gathered(proj_out[:, 1])
    near = jnp.concatenate([earlier, own[:, width:]], axis=0)
    key1, value1 = near[:, :width], near[:, width:]
    attended1, stats1 = near_forward(query1, key1, value1)
    full1 = chain_sum(nt(attended1, w_out1), full0, turns=1)
    branch1, saved1 = feed_forward(full1, gain[1], w_pair1, w_down1)
    full2 = chain_sum(branch1, full1)
    normed3, local_cache, normed4, query2 = project(
        full2, w_cross, [(gain[2], 0, 2 * width), (gain[3], 2 * width, width)]
    )
    local_cache, own_dout, w_out2, own_down2 = lax.optimization_barrier(
        (local_cache, cotangent, w_out2, ffn_down[:, 1])
    )
    cache_kv = gathered(local_cache)
    dfull4 = spread(own_dout)
    query2 = swapped(query2)
    query2, dfull4 = lax.optimization_barrier((query2, dfull4))
    w_down2 = gathered(pad_columns(own_down2))
    attended2, stats2 = far_forward(query2, cache_kv)
    own_attended2 = swapped(attended2)
    own_attended2, own_pair2 = lax.optimization_barrier((own_attended2, own_pair2))
    w_pair2 = gathered(own_pair2)
    full3 = chain_sum(nt(own_attended2, w_out2), full2, turns=2)
    branch2, saved2 = feed_forward(full3, gain[4], w_pair2, w_down2)

    dpart, pairs_feed2, grad_gain4 = feed_backward(dfull4, gain[4], w_pair2, w_down2, saved2)
    dfull3 = chain_sum(dpart, dfull4)
    dattended2 = swapped(nn(dfull3, w_out2).astype(bf16))
    dquery2, dcache = far_backward(query2, cache_kv, dattended2, attended2, stats2)
    dcache, branch2, pairs_feed2 = lax.optimization_barrier((dcache, branch2, pairs_feed2))
    dquery2 = swapped(dquery2)
    dcache = lax.psum_scatter(dcache, "seq", scatter_dimension=0, tiled=True)
    output = chain_sum(branch2, full3, own_only=True)
    grad_feed2 = gradients(pairs_feed2)
    dcache, output, grad_feed2 = lax.optimization_barrier((dcache, output, grad_feed2))
    grad_feed2 = scattered(grad_feed2)
    dpart, grad_gain2, grad_gain3 = project_back(
        full2,
        w_cross,
        [(gain[2], 0, 2 * width, dcache), (gain[3], 2 * width, width, dquery2)],
    )
    dpart, (grad_cross,) = together(
        dpart,
        (gradients([(normed3, dcache), (normed4, dquery2), (dfull3, own_attended2)]),),
    )
    grad_cross = scattered(grad_cross)
    dfull2 = chain_sum(dpart, dfull3, turns=3)
    dpart, pairs_feed1, grad_gain1 = feed_backward(dfull2, gain[1], w_pair1, w_down1, saved1)
    dpart, (grad_feed1,) = together(dpart, (gradients(pairs_feed1),))
    grad_feed1 = scattered(grad_feed1)
    dpart, grad_cross, grad_feed2 = lax.optimization_barrier((dpart, grad_cross, grad_feed2))
    dfull1 = chain_sum(dpart, dfull2)
    dattended1 = nn(dfull1, w_out1).astype(bf16)
    dquery1, dkey1, dvalue1 = near_backward(query1, key1, value1, dattended1, attended1, stats1)
    dnear = jnp.concatenate([dkey1, dvalue1], axis=1)
    returned = shifted(dnear[:rows].astype(bf16), "seq", -1).astype(f32)
    grad_first = gradients([(normed1, dquery1), (dfull1, attended1)])
    dpairs = (dnear[rows:] + returned).astype(bf16)
    dself = jnp.concatenate([dquery1, dpairs], axis=1)
    dself, grad_feed1 = lax.optimization_barrier((dself, grad_feed1))
    dpart, grad_gain0 = project_back(full0, packed, [(gain[0], 0, 3 * width, dself)])
    all_gains = [grad_gain0, grad_gain1, grad_gain2, grad_gain3, grad_gain4]
    all_gains = pad_columns(jnp.concatenate(all_gains, axis=0).T.astype(bf16))
    dpart, (grad_self,) = together(
        dpart, (gradients([(normed1, dself[:, width:])], (grad_first, all_gains)),)
    )
    grad_self = scattered(grad_self)
    grad_inputs, grad_self = lax.optimization_barrier(
        (chain_sum(dpart, dfull1, own_only=True), grad_self)
    )
    total_gains = small_sum(grad_self[:, 4 * width :].astype(f32))[:, :5]
    grad_cache = grad_cross[:, : 2 * width].reshape(depth, heads, 2, HEAD_DIM)
    grad_cache = grad_cache.transpose(0, 2, 1, 3).reshape(depth, 2 * width)
    grad_in = jnp.concatenate(
        [
            grad_self[:, 2 * width : 3 * width],
            grad_self[:, : 2 * width],
            grad_cache,
            grad_cross[:, 2 * width : 3 * width],
        ],
        axis=1,
    )
    grad_out = [grad_self[:, 3 * width : 4 * width], grad_cross[:, 3 * width :]]
    grad_ffn = [
        grads[:, start : start + hidden_width]
        for grads in (grad_feed1, grad_feed2)
        for start in (0, half)
    ]
    grad_down = [grads[:, 2 * half : 2 * half + hidden_width] for grads in (grad_feed1, grad_feed2)]
    return (
        output,
        grad_inputs,
        grad_in.astype(f32).reshape(depth, 6, width),
        jnp.stack(grad_out, axis=1).astype(f32),
        jnp.stack(grad_ffn, axis=1).astype(f32),
        jnp.stack(grad_down, axis=1).astype(f32),
        total_gains,
    )


def solution(mesh):
    wide = P("seq", "tensor")
    weight = P("seq", None, "tensor")
    gain = P("seq", None)
    return jax.shard_map(
        shards,
        mesh=mesh,
        in_specs=(wide, wide, weight, weight, weight, weight, gain),
        out_specs=(wide, wide, weight, weight, weight, weight, gain),
        check_vma=False,
    )
```

```python
import functools

import jax
import jax.numpy as jnp
from jax import lax
from jax.experimental import pallas as pl
from jax.experimental.pallas import tpu as pltpu
from jax.sharding import PartitionSpec as P

HEAD_DIM = 128
WINDOW = 1024
SCALE = HEAD_DIM ** (-0.5)
SCALE2 = SCALE * 1.4426950408889634

epsilon = 1e-06
floor_score = -1e30
f32 = jnp.float32
bf16 = jnp.bfloat16
MIB = 1 << 20


def nt(left, right):
    return lax.dot_general(left, right, (((1,), (1,)), ((), ())), preferred_element_type=f32)


def tn(left, right):
    return lax.dot_general(left, right, (((0,), (0,)), ((), ())), preferred_element_type=f32)


def nn(left, right):
    return lax.dot_general(left, right, (((1,), (0,)), ((), ())), preferred_element_type=f32)


def row_dot(dout, out):
    product = dout.astype(f32) * out.astype(f32)
    return jnp.sum(product.T, axis=0, keepdims=True)


def near_allowed(span, size, start, rows):
    key = lax.broadcasted_iota(jnp.int32, (span, size), 0)
    query = lax.broadcasted_iota(jnp.int32, (span, size), 1)
    first = jnp.where(lax.axis_index("seq") == 0, rows - start, 0)
    return (key >= jnp.maximum(query + 1, first)) & (key <= query + WINDOW)


def near_forward_kernel(rows, q_ref, k_ref, v_ref, o_ref, stat_ref):
    size = q_ref.shape[0]
    span = WINDOW + size
    start = pl.multiple_of(pl.program_id(1) * size + (rows - WINDOW), size)
    allowed = near_allowed(span, size, start, rows)
    scores = nt(k_ref[pl.ds(start, span), :], q_ref[...]) * SCALE2
    scores = jnp.where(allowed, scores, floor_score)
    top = jnp.max(scores, axis=0, keepdims=True)
    weight = jnp.exp2(scores - top)
    total = jnp.sum(weight, axis=0, keepdims=True)
    mixed = tn(v_ref[pl.ds(start, span), :], weight.astype(bf16)) / total
    o_ref[...] = mixed.T.astype(bf16)
    stat_ref[0] = top + jnp.log2(total)


def near_forward(queries, keys, values):
    rows, width = queries.shape
    heads, size = width // HEAD_DIM, min(256, rows)
    own = pl.BlockSpec((size, HEAD_DIM), lambda h, b: (b, h))
    span = pl.BlockSpec((keys.shape[0], HEAD_DIM), lambda h, b: (0, h))
    stat = pl.BlockSpec((1, 1, size), lambda h, b: (h, 0, b))
    pairs = heads * rows * (WINDOW + size)
    return pl.pallas_call(
        functools.partial(near_forward_kernel, rows),
        grid=(heads, rows // size),
        in_specs=[own, span, span],
        out_specs=[own, stat],
        out_shape=[
            jax.ShapeDtypeStruct((rows, width), bf16),
            jax.ShapeDtypeStruct((heads, 1, rows), f32),
        ],
        compiler_params=pltpu.CompilerParams(vmem_limit_bytes=40 * MIB),
        cost_estimate=pl.CostEstimate(
            flops=pairs * 4 * HEAD_DIM * 2, bytes_accessed=rows * width * 12, transcendentals=pairs
        ),
        name="near_forward",
    )(queries, keys, values)


def near_backward_kernel(rows, q_ref, k_ref, v_ref, do_ref, o_ref, stat_ref, dq_ref, dk_ref, dv_ref):
    size = q_ref.shape[0]
    span = WINDOW + size
    start = pl.multiple_of(pl.program_id(1) * size + (rows - WINDOW), size)

    @pl.when(pl.program_id(1) == 0)
    def clear():
        dk_ref[...] = jnp.zeros_like(dk_ref)
        dv_ref[...] = jnp.zeros_like(dv_ref)

    place = pl.ds(start, span)
    queries, dout = q_ref[...], do_ref[...]
    keys, values = k_ref[place, :], v_ref[place, :]
    inner = row_dot(dout, o_ref[...])
    allowed = near_allowed(span, size, start, rows)
    scores = nt(keys, queries) * SCALE2 - stat_ref[0]
    weight = jnp.exp2(jnp.where(allowed, scores, floor_score))
    dscore = (weight * (nt(values, dout) - inner)).astype(bf16)
    dv_ref[place, :] += nn(weight.astype(bf16), dout)
    dk_ref[place, :] += nn(dscore, queries) * SCALE
    dq_ref[...] = (tn(keys, dscore) * SCALE).T.astype(bf16)


def near_backward(queries, keys, values, dresult, result, stats):
    rows, width = queries.shape
    heads, size = width // HEAD_DIM, min(256, rows)
    own = pl.BlockSpec((size, HEAD_DIM), lambda h, b: (b, h))
    span = pl.BlockSpec((keys.shape[0], HEAD_DIM), lambda h, b: (0, h))
    stat = pl.BlockSpec((1, 1, size), lambda h, b: (h, 0, b))
    pairs = heads * rows * (WINDOW + size)
    return pl.pallas_call(
        functools.partial(near_backward_kernel, rows),
        grid=(heads, rows // size),
        in_specs=[own, span, span, own, own, stat],
        out_specs=[own, span, span],
        out_shape=[
            jax.ShapeDtypeStruct((rows, width), bf16),
            jax.ShapeDtypeStruct(keys.shape, f32),
            jax.ShapeDtypeStruct(keys.shape, f32),
        ],
        compiler_params=pltpu.CompilerParams(vmem_limit_bytes=40 * MIB),
        cost_estimate=pl.CostEstimate(
            flops=pairs * 10 * HEAD_DIM * 2, bytes_accessed=rows * width * 32, transcendentals=pairs
        ),
        name="near_backward",
    )(queries, keys, values, dresult, result, stats)


def far_place(block):
    mine, count = lax.axis_index("seq"), lax.axis_size("seq")
    return jnp.where(block == 0, 2 * mine, 2 * count - 1 - 2 * mine)


def triangle(size, start, width):
    key = lax.broadcasted_iota(jnp.int32, (size, width), 0)
    query = lax.broadcasted_iota(jnp.int32, (size, width), 1)
    return key <= query + start


def query_parts(size):
    return [(start, size // 2) for start in (0, size // 2)]


def far_forward_kernel(q_ref, kv_ref, o_ref, stat_ref, top_ref, sum_ref, acc_ref):
    size = q_ref.shape[0]
    last = far_place(pl.program_id(1))
    top_ref[...] = jnp.full_like(top_ref, floor_score)
    sum_ref[...] = jnp.zeros_like(sum_ref)
    acc_ref[...] = jnp.zeros_like(acc_ref)

    def step(index, masked):
        place = pl.ds(pl.multiple_of(index * size, size), size)
        keys, values = kv_ref[place, :HEAD_DIM], kv_ref[place, HEAD_DIM:]
        parts = query_parts(size)
        all_scores = [nt(keys, q_ref[start : start + width, :]) for start, width in parts]
        for (start, width), scores in zip(parts, all_scores):
            own = slice(start, start + width)
            scores = scores * SCALE2
            if masked:
                scores = jnp.where(triangle(size, start, width), scores, floor_score)
            before = top_ref[:, own]
            top = jnp.maximum(before, jnp.max(scores, axis=0, keepdims=True))
            weight = jnp.exp2(scores - top)
            fade = jnp.exp2(before - top)
            top_ref[:, own] = top
            sum_ref[:, own] = sum_ref[:, own] * fade + jnp.sum(weight, axis=0, keepdims=True)
            acc_ref[:, own] = acc_ref[:, own] * fade + tn(values, weight.astype(bf16))

    @pl.loop(0, last)
    def earlier(index):
        step(index, False)

    step(last, True)
    o_ref[...] = (acc_ref[...] / sum_ref[...]).T.astype(bf16)
    stat_ref[0] = top_ref[...] + jnp.log2(sum_ref[...])


def far_forward(queries, pairs_kv):
    rows, width = queries.shape
    heads, size = width // HEAD_DIM, rows // 2
    own = pl.BlockSpec((size, HEAD_DIM), lambda h, b: (b, h))
    whole = pl.BlockSpec((pairs_kv.shape[0], 2 * HEAD_DIM), lambda h, b: (0, h))
    stat = pl.BlockSpec((1, 1, size), lambda h, b: (h, 0, b))
    pairs = heads * rows * pairs_kv.shape[0] // 2
    return pl.pallas_call(
        far_forward_kernel,
        grid=(heads, 2),
        in_specs=[own, whole],
        out_specs=[own, stat],
        out_shape=[
            jax.ShapeDtypeStruct((rows, width), bf16),
            jax.ShapeDtypeStruct((heads, 1, rows), f32),
        ],
        scratch_shapes=[
            pltpu.VMEM((1, size), f32),
            pltpu.VMEM((1, size), f32),
            pltpu.VMEM((HEAD_DIM, size), f32),
        ],
        compiler_params=pltpu.CompilerParams(vmem_limit_bytes=48 * MIB),
        cost_estimate=pl.CostEstimate(
            flops=pairs * 4 * HEAD_DIM * 2,
            bytes_accessed=pairs_kv.shape[0] * width * 4,
            transcendentals=pairs,
        ),
        name="far_forward",
    )(queries, pairs_kv)


def far_backward_kernel(
    q_ref, kv_ref, do_ref, o_ref, stat_ref, dq_ref, dkv_ref, dq_acc, dk_acc, dv_acc
):
    size = q_ref.shape[0]
    block = pl.program_id(1)
    last = far_place(block)

    @pl.when(block == 0)
    def clear():
        dk_acc[...] = jnp.zeros_like(dk_acc)
        dv_acc[...] = jnp.zeros_like(dv_acc)

    dq_acc[...] = jnp.zeros_like(dq_acc)
    inner = row_dot(do_ref[...], o_ref[...])

    def step(index, masked):
        place = pl.ds(pl.multiple_of(index * size, size), size)
        keys, values = kv_ref[place, :HEAD_DIM], kv_ref[place, HEAD_DIM:]
        parts = []
        for start, width in query_parts(size):
            own = slice(start, start + width)
            queries, dout = q_ref[own, :], do_ref[own, :]
            parts.append((start, width, own, queries, dout, nt(keys, queries), nt(values, dout)))
        dvalues, dkeys = [], []
        for start, width, own, queries, dout, scores, dweight in parts:
            scores = scores * SCALE2 - stat_ref[0, :, own]
            if masked:
                scores = jnp.where(triangle(size, start, width), scores, floor_score)
            weight = jnp.exp2(scores)
            dscore = (weight * (dweight - inner[:, own])).astype(bf16)
            dvalues.append(nn(weight.astype(bf16), dout))
            dkeys.append(nn(dscore, queries))
            dq_acc[:, own] += tn(keys, dscore)
        dv_acc[place, :] += dvalues[0] + dvalues[1]
        dk_acc[place, :] += dkeys[0] + dkeys[1]

    @pl.loop(0, last)
    def earlier(index):
        step(index, False)

    step(last, True)
    dq_ref[...] = (dq_acc[...] * SCALE).T.astype(bf16)

    @pl.when(block == 1)
    def leave():
        dkv_ref[:, :HEAD_DIM] = (dk_acc[...] * SCALE).astype(bf16)
        dkv_ref[:, HEAD_DIM:] = dv_acc[...].astype(bf16)


def far_backward(queries, pairs_kv, dresult, result, stats):
    rows, width = queries.shape
    heads, size = width // HEAD_DIM, rows // 2
    tokens = pairs_kv.shape[0]
    own = pl.BlockSpec((size, HEAD_DIM), lambda h, b: (b, h))
    whole = pl.BlockSpec((tokens, 2 * HEAD_DIM), lambda h, b: (0, h))
    stat = pl.BlockSpec((1, 1, size), lambda h, b: (h, 0, b))
    pairs = heads * rows * tokens // 2
    return pl.pallas_call(
        far_backward_kernel,
        grid=(heads, 2),
        in_specs=[own, whole, own, own, stat],
        out_specs=[own, whole],
        out_shape=[
            jax.ShapeDtypeStruct((rows, width), bf16),
            jax.ShapeDtypeStruct(pairs_kv.shape, bf16),
        ],
        scratch_shapes=[
            pltpu.VMEM((HEAD_DIM, size), f32),
            pltpu.VMEM((tokens, HEAD_DIM), f32),
            pltpu.VMEM((tokens, HEAD_DIM), f32),
        ],
        compiler_params=pltpu.CompilerParams(vmem_limit_bytes=60 * MIB),
        cost_estimate=pl.CostEstimate(
            flops=pairs * 10 * HEAD_DIM * 2,
            bytes_accessed=tokens * width * 8,
            transcendentals=pairs,
        ),
        name="far_backward",
    )(queries, pairs_kv, dresult, result, stats)


def greet_neighbours(mine, count, partner=None):
    barrier = pltpu.get_barrier_semaphore()
    sides = ((-1, mine > 0), (1, mine < count - 1))
    if partner is not None:
        pl.semaphore_signal(
            barrier, inc=1, device_id={"seq": partner}, device_id_type=pl.DeviceIdType.MESH
        )
    for side, present in sides:

        @pl.when(present)
        def greet():
            pl.semaphore_signal(
                barrier,
                inc=1,
                device_id={"tensor": mine + side},
                device_id_type=pl.DeviceIdType.MESH,
            )

    others = 0 if partner is None else 1
    pl.semaphore_wait(barrier, others + sum(present.astype(jnp.int32) for _, present in sides))


def chain_kernel(chunk, turns, own_only, part_ref, base_ref, *refs):
    if own_only:
        own_ref, out_ref, *refs = refs
    else:
        out_ref, *refs = refs
    sum_ref, rs_send, rs_recv, ag_send, ag_recv, *refs = refs
    turn = refs[0] if turns else None
    count = lax.axis_size("tensor")
    mine = lax.axis_index("tensor")
    rows, depth = part_ref.shape
    half, pieces, slack = depth // 2, rows // chunk, 2
    hops = count // 2 - 1 if own_only else count - 1
    ticks = pieces + slack * (count - 1 + hops)
    core = lax.rem(lax.axis_index("seq"), 2)
    partner = lax.axis_index("seq") + 1 - 2 * core if turns else None
    greet_neighbours(mine, count, partner)
    if turns:

        @pl.when(core == 1)
        def follow():
            pl.semaphore_wait(turn, 1)

    flows = [(0, mine, -1), (1, count - 1 - mine, 1)]

    def area(flow, piece):
        return (pl.ds(pl.multiple_of(piece * chunk, chunk), chunk), pl.ds(flow * half, half))

    def inward(flow, step, piece, source):
        rows_cols = area(flow, piece)
        return pltpu.make_async_remote_copy(
            src_ref=source.at[rows_cols],
            dst_ref=sum_ref.at[rows_cols],
            send_sem=rs_send.at[flow, piece],
            recv_sem=rs_recv.at[flow, piece],
            device_id={"tensor": mine + step},
            device_id_type=pl.DeviceIdType.MESH,
        )

    def outward(flow, step, piece, hop):
        rows_cols = area(flow, piece)
        if own_only:
            width = depth // count
            start, length = (hop + 1) * width, half - (hop + 1) * width
            rows_cols = (rows_cols[0], pl.ds(half if flow else start, length))
        return pltpu.make_async_remote_copy(
            src_ref=out_ref.at[rows_cols],
            dst_ref=out_ref.at[rows_cols],
            send_sem=ag_send.at[flow, piece],
            recv_sem=ag_recv.at[flow, piece],
            device_id={"tensor": mine - step},
            device_id_type=pl.DeviceIdType.MESH,
        )

    @pl.loop(0, ticks)
    def beat(tick):
        if turns:

            @pl.when((core == 0) & (tick == ticks * 7 // 8))
            def lead():
                pl.semaphore_signal(
                    turn, inc=1, device_id={"seq": partner}, device_id_type=pl.DeviceIdType.MESH
                )

        for flow, far, step in flows:
            piece = tick - slack * (count - 1 - far)
            live = (piece >= 0) & (piece < pieces)

            @pl.when(live & (far == count - 1))
            def leaf():
                inward(flow, step, piece, part_ref).start()

            @pl.when(live & (far < count - 1))
            def arrived():
                inward(flow, step, piece, sum_ref).wait_recv()

            @pl.when(live & (far < count - 1) & (far > 0))
            def middle():
                rows_cols = area(flow, piece)
                sum_ref[rows_cols] = (
                    sum_ref[rows_cols].astype(f32) + part_ref[rows_cols].astype(f32)
                ).astype(bf16)
                inward(flow, step, piece, sum_ref).start()

            @pl.when(live & (far == 0))
            def root():
                rows_cols = area(flow, piece)
                out_ref[rows_cols] = (
                    sum_ref[rows_cols].astype(f32)
                    + part_ref[rows_cols].astype(f32)
                    + base_ref[rows_cols].astype(f32)
                ).astype(bf16)
                if hops > 0:
                    outward(flow, step, piece, 0).start()

        for flow, far, step in flows:
            piece = tick - slack * (count - 1 + far)
            live = (piece >= 0) & (piece < pieces)
            for hop in range(hops) if own_only else (0,):

                @pl.when(live & ((far == hop + 1) if own_only else (far > 0)))
                def landed():
                    outward(flow, step, piece, hop).wait_recv()

                if own_only and hop + 1 == hops:
                    continue

                @pl.when(live & ((far == hop + 1) if own_only else (far > 0) & (far < hops)))
                def forward():
                    outward(flow, step, piece, hop + 1).start()

    if own_only:
        width = depth // count
        own_ref[...] = out_ref[:, pl.ds(pl.multiple_of(mine * width, width), width)].astype(f32)

    @pl.loop(0, pieces)
    def finish(piece):
        for flow, far, step in flows:

            @pl.when(far > 0)
            def sent_in():
                inward(flow, step, piece, sum_ref).wait_send()

            for hop in range(hops) if own_only else (0,):

                @pl.when((far == hop) if own_only else (far < hops))
                def sent_out():
                    outward(flow, step, piece, hop).wait_send()


def chain_sum(partial_value, base, turns=0, own_only=False, brief=False):
    turns = turns if lax.axis_size("seq") % 2 == 0 else 0
    rows, depth = base.shape
    chunk = 32
    pieces = rows // chunk
    own_width = depth // lax.axis_size("tensor") if own_only else depth
    whole = pl.BlockSpec(memory_space=pltpu.VMEM)
    return pl.pallas_call(
        functools.partial(chain_kernel, chunk, turns, own_only),
        in_specs=[whole, whole],
        out_specs=whole,
        out_shape=jax.ShapeDtypeStruct((rows, own_width), f32 if own_only else bf16),
        scratch_shapes=[pltpu.VMEM((rows, depth), bf16)] * (2 if own_only else 1)
        + [pltpu.SemaphoreType.DMA((2, pieces))] * 4
        + [pltpu.SemaphoreType.REGULAR] * (turns > 0),
        compiler_params=pltpu.CompilerParams(
            collective_id=1 + turns if turns else 6 * own_only, has_side_effects=True, vmem_limit_bytes=32 * MIB
        ),
        cost_estimate=pl.CostEstimate(
            flops=10**6 if brief else 10**11, bytes_accessed=10**6, transcendentals=0
        ),
        name="chain_sum_turns" if turns else "chain_own" if own_only else "chain_sum",
    )(partial_value.astype(bf16), base)


def spread_kernel(chunk, own_ref, out_ref, send_sem, recv_sem):
    count = lax.axis_size("tensor")
    mine = lax.axis_index("tensor")
    rows, width = own_ref.shape
    pieces = rows // chunk
    greet_neighbours(mine, count)

    def copy(way, side, hop, piece):
        source = jnp.clip(mine - side * hop, 0, count - 1)
        place = (
            pl.ds(pl.multiple_of(piece * chunk, chunk), chunk),
            pl.ds(pl.multiple_of(source * width, width), width),
        )
        return pltpu.make_async_remote_copy(
            src_ref=out_ref.at[place],
            dst_ref=out_ref.at[place],
            send_sem=send_sem.at[way, hop, piece],
            recv_sem=recv_sem.at[way, hop, piece],
            device_id={"tensor": jnp.clip(mine + side, 0, count - 1)},
            device_id_type=pl.DeviceIdType.MESH,
        )

    def landing(way, side, hop, piece):
        source = jnp.clip(mine - side * hop, 0, count - 1)
        place = (
            pl.ds(pl.multiple_of(piece * chunk, chunk), chunk),
            pl.ds(pl.multiple_of(source * width, width), width),
        )
        return pltpu.make_async_remote_copy(
            src_ref=out_ref.at[place],
            dst_ref=out_ref.at[place],
            send_sem=send_sem.at[way, hop - 1, piece],
            recv_sem=recv_sem.at[way, hop - 1, piece],
            device_id={"tensor": jnp.clip(mine + side, 0, count - 1)},
            device_id_type=pl.DeviceIdType.MESH,
        )

    ways = [(0, 1), (1, -1)]
    out_ref[:, pl.ds(pl.multiple_of(mine * width, width), width)] = own_ref[...].astype(bf16)

    for hop in range(count):

        @pl.loop(0, pieces)
        def pass_on(piece):
            for way, side in ways:
                source, target = mine - side * hop, mine + side
                held = (source >= 0) & (source < count)

                if hop > 0:

                    @pl.when(held)
                    def landed():
                        landing(way, side, hop, piece).wait_recv()

                if hop < count - 1:

                    @pl.when(held & (target >= 0) & (target < count))
                    def forward():
                        copy(way, side, hop, piece).start()

    for hop in range(count - 1):

        @pl.loop(0, pieces)
        def finish(piece):
            for way, side in ways:
                source, target = mine - side * hop, mine + side

                @pl.when((source >= 0) & (source < count) & (target >= 0) & (target < count))
                def sent():
                    copy(way, side, hop, piece).wait_send()


def spread(own_rows):
    rows, width = own_rows.shape
    count, chunk = lax.axis_size("tensor"), 128
    whole = pl.BlockSpec(memory_space=pltpu.VMEM)
    return pl.pallas_call(
        functools.partial(spread_kernel, chunk),
        in_specs=[whole],
        out_specs=whole,
        out_shape=jax.ShapeDtypeStruct((rows, width * count), bf16),
        scratch_shapes=[pltpu.SemaphoreType.DMA((2, count - 1, rows // chunk))] * 2,
        compiler_params=pltpu.CompilerParams(
            collective_id=1, has_side_effects=True, vmem_limit_bytes=24 * MIB
        ),
        cost_estimate=pl.CostEstimate(
            flops=7 * 10**10, bytes_accessed=rows * width * 20, transcendentals=0
        ),
        name="spread",
    )(own_rows)


def small_kernel(own_ref, out_ref, land_ref, send_sem, recv_sem):
    count = lax.axis_size("tensor")
    mine = lax.axis_index("tensor")
    barrier = pltpu.get_barrier_semaphore()
    others = [lax.rem(mine + step, count) for step in range(1, count)]
    for other in others:
        pl.semaphore_signal(
            barrier, inc=1, device_id={"tensor": other}, device_id_type=pl.DeviceIdType.MESH
        )
    pl.semaphore_wait(barrier, count - 1)
    copies = [
        pltpu.make_async_remote_copy(
            src_ref=own_ref,
            dst_ref=land_ref.at[mine],
            send_sem=send_sem.at[slot],
            recv_sem=recv_sem.at[slot],
            device_id={"tensor": other},
            device_id_type=pl.DeviceIdType.MESH,
        )
        for slot, other in enumerate(others)
    ]
    for copy in copies:
        copy.start()
    land_ref[mine] = own_ref[...]
    for copy in copies:
        copy.wait()
    total = land_ref[0]
    for place in range(1, count):
        total = total + land_ref[place]
    out_ref[...] = total


def small_sum(value):
    count = lax.axis_size("tensor")
    whole = pl.BlockSpec(memory_space=pltpu.VMEM)
    return pl.pallas_call(
        small_kernel,
        in_specs=[whole],
        out_specs=whole,
        out_shape=jax.ShapeDtypeStruct(value.shape, f32),
        scratch_shapes=[pltpu.VMEM((count, *value.shape), f32)]
        + [pltpu.SemaphoreType.DMA((count - 1,))] * 2,
        compiler_params=pltpu.CompilerParams(collective_id=5, has_side_effects=True),
        cost_estimate=pl.CostEstimate(flops=10**9, bytes_accessed=value.size * 8, transcendentals=0),
        name="small_sum",
    )(value)


def shifted(block, axis, distance):
    devices = range(lax.axis_size(axis))
    route = [(i - distance, i) for i in devices if i - distance in devices]
    return lax.ppermute(block, axis, route)


def swapped(block):
    count, half = lax.axis_size("seq"), block.shape[0] // 2
    other = lax.ppermute(block[half:], "seq", [(i, count - 1 - i) for i in range(count)])
    return jnp.concatenate([block[:half], other], axis=0)


def gathered(weight):
    return lax.all_gather(weight, "seq", axis=0, tiled=True)


def scattered(grad):
    return lax.psum_scatter(grad.astype(bf16), "seq", scatter_dimension=0, tiled=True)


def together(value, grads):
    return lax.optimization_barrier((value.astype(bf16), tuple(g.astype(bf16) for g in grads)))


def inverse_rms(rows):
    return lax.rsqrt(jnp.mean(rows * rows, axis=1, keepdims=True) + epsilon)


def norm_back(rows, gain_row, gradient):
    inverse = inverse_rms(rows)
    scaled = gradient * gain_row
    cubed = inverse * inverse * inverse
    dfull = inverse * scaled - rows * cubed * jnp.mean(scaled * rows, axis=1, keepdims=True)
    return (dfull, jnp.sum(gradient * rows * inverse, axis=0, keepdims=True))


def row_block(size, width):
    return pl.BlockSpec((size, width), lambda i: (i, 0))


def resident(array):
    return pl.BlockSpec(array.shape, lambda i: (0, 0), pipeline_mode=pl.Buffered(1))


def blocks_call(kernel, name, rows, size, ins, outs, flops, weights=()):
    in_specs = [row_block(size, x.shape[1]) if cut else resident(x) for x, cut in ins]
    in_specs += [pl.BlockSpec(memory_space=pl.ANY) for _ in weights]
    scratch = [pltpu.VMEM(x.shape, x.dtype) for x in weights]
    if weights:
        scratch.append(pltpu.SemaphoreType.DMA((3,)))
    out_specs = [
        row_block(size, shape[1]) if cut else pl.BlockSpec(shape, lambda i: (0, 0))
        for shape, _, cut in outs
    ]
    return pl.pallas_call(
        kernel,
        grid=(rows // size,),
        in_specs=in_specs,
        out_specs=out_specs,
        out_shape=[jax.ShapeDtypeStruct(shape, kind) for shape, kind, _ in outs],
        compiler_params=pltpu.CompilerParams(vmem_limit_bytes=56 * MIB),
        cost_estimate=pl.CostEstimate(
            flops=flops, bytes_accessed=sum(x.size * 2 for x, _ in ins), transcendentals=0
        ),
        scratch_shapes=scratch,
        name=name,
    )(*[x for x, _ in ins], *weights)


def project_kernel(parts, full_ref, weight_ref, *refs):
    gains, outs = refs[: len(parts)], refs[len(parts) :]
    rows = full_ref[...].astype(f32)
    scaled = rows * inverse_rms(rows)
    for place, (start, width) in enumerate(parts):
        normed = (scaled * gains[place][...]).astype(bf16)
        outs[2 * place][...] = normed
        outs[2 * place + 1][...] = nn(normed, weight_ref[:, start : start + width]).astype(bf16)


def project(full, weight, parts):
    rows, depth = full.shape
    outs = []
    for _, _, width in parts:
        outs += [((rows, depth), bf16, True), ((rows, width), bf16, True)]
    return blocks_call(
        functools.partial(project_kernel, [part[1:] for part in parts]),
        "project",
        rows,
        min(256, rows),
        [(full, True), (weight, False)] + [(gain, False) for gain, _, _ in parts],
        outs,
        2 * rows * depth * sum(width for _, _, width in parts),
    )


def project_back_kernel(parts, full_ref, weight_ref, *refs):
    count = len(parts)
    gains, grads, dfull_ref, dgains = refs[:count], refs[count : 2 * count], refs[2 * count], refs[2 * count + 1 :]

    @pl.when(pl.program_id(0) == 0)
    def clear():
        for ref in dgains:
            ref[...] = jnp.zeros_like(ref)

    rows = full_ref[...].astype(f32)
    total = jnp.zeros_like(rows)
    for place, (start, width) in enumerate(parts):
        dnormed = nt(grads[place][...], weight_ref[:, start : start + width])
        dfull, dgain = norm_back(rows, gains[place][...], dnormed)
        total = total + dfull
        dgains[place][...] += dgain
    dfull_ref[...] = total.astype(bf16)


def project_back(full, weight, parts):
    rows, depth = full.shape
    return blocks_call(
        functools.partial(project_back_kernel, [part[1:3] for part in parts]),
        "project_back",
        rows,
        min(256, rows),
        [(full, True), (weight, False)]
        + [(part[0], False) for part in parts]
        + [(part[3], True) for part in parts],
        [((rows, depth), bf16, True)] + [((1, depth), f32, False)] * len(parts),
        2 * rows * depth * sum(part[2] for part in parts),
    )


def weight_copies(pair_hbm, down_hbm, pair_weight, down_weight, sems):
    half = down_weight.shape[1]
    gate, upward = pl.ds(0, half), pl.ds(half, half)
    return [
        pltpu.make_async_copy(pair_hbm.at[:, gate], pair_weight.at[:, gate], sems.at[0]),
        pltpu.make_async_copy(pair_hbm.at[:, upward], pair_weight.at[:, upward], sems.at[1]),
        pltpu.make_async_copy(down_hbm, down_weight, sems.at[2]),
    ]


def at_first(action):
    pl.when(pl.program_id(0) == 0)(action)


def feed_forward_kernel(
    full_ref, gain_ref, pair_hbm, down_hbm, branch_ref, normed_ref, pair_ref, hidden_ref, *weights
):
    pair_weight, down_weight, sems = weights
    copies = weight_copies(pair_hbm, down_hbm, pair_weight, down_weight, sems)
    half = hidden_ref.shape[1]

    @at_first
    def fetch():
        for copy in copies:
            copy.start()

    rows = full_ref[...].astype(f32)
    normed = (rows * inverse_rms(rows) * gain_ref[...]).astype(bf16)
    normed_ref[...] = normed
    at_first(copies[0].wait)
    gate = nn(normed, pair_weight[:, :half])
    at_first(copies[1].wait)
    upward = nn(normed, pair_weight[:, half:])
    pair_ref[:, :half] = gate.astype(bf16)
    pair_ref[:, half:] = upward.astype(bf16)
    hidden = (gate * jax.nn.sigmoid(gate) * upward).astype(bf16)
    hidden_ref[...] = hidden
    at_first(copies[2].wait)
    branch_ref[...] = nt(hidden, down_weight[...]).astype(bf16)


def feed_forward(full, gain, weight_pair, weight_down):
    rows, depth = full.shape
    half = weight_down.shape[1]
    branch, normed, pair, hidden = blocks_call(
        feed_forward_kernel,
        "feed_forward",
        rows,
        min(512, rows),
        [(full, True), (gain, False)],
        [
            ((rows, depth), bf16, True),
            ((rows, depth), bf16, True),
            ((rows, 2 * half), bf16, True),
            ((rows, half), bf16, True),
        ],
        6 * rows * depth * half,
        (weight_pair, weight_down),
    )
    return (branch, (full, normed, pair, hidden))


def feed_backward_kernel(
    dout_ref, full_ref, pair_ref, gain_ref, pair_hbm, down_hbm, dfull_ref, dpair_ref, dgain_ref, *weights
):
    pair_weight, down_weight, sems = weights
    copies = weight_copies(pair_hbm, down_hbm, pair_weight, down_weight, sems)
    half = down_weight.shape[1]

    @at_first
    def fetch():
        for copy in copies[::-1]:
            copy.start()
        dgain_ref[...] = jnp.zeros_like(dgain_ref)
        copies[2].wait()

    dhidden = nn(dout_ref[...], down_weight[...])
    gate, upward = pair_ref[:, :half].astype(f32), pair_ref[:, half:].astype(f32)
    sigma = jax.nn.sigmoid(gate)
    dpair_ref[:, :half] = (dhidden * upward * sigma * (1.0 + gate * (1.0 - sigma))).astype(bf16)
    dpair_ref[:, half:] = (dhidden * gate * sigma).astype(bf16)

    @at_first
    def have_pair():
        copies[0].wait()
        copies[1].wait()

    dfull, dgain = norm_back(
        full_ref[...].astype(f32), gain_ref[...], nt(dpair_ref[...], pair_weight[...])
    )
    dfull_ref[...] = dfull.astype(bf16)
    dgain_ref[...] += dgain


def feed_backward(dbranch, gain, weight_pair, weight_down, saved):
    full, normed, pair, hidden = saved
    rows, depth = full.shape
    half = weight_down.shape[1]
    dfull, dpair, grad_gain = blocks_call(
        feed_backward_kernel,
        "feed_backward",
        rows,
        min(512, rows),
        [
            (dbranch, True),
            (full, True),
            (pair, True),
            (gain, False),
        ],
        [((rows, depth), bf16, True), ((rows, 2 * half), bf16, True), ((1, depth), f32, False)],
        6 * rows * depth * half,
        (weight_pair, weight_down),
    )
    return (dfull, [(normed, dpair), (dbranch, hidden)], grad_gain)


def gradients_kernel(count, *refs):
    lefts, rights, extra, out_ref = refs[:count], refs[count : 2 * count], refs[2 * count : -1], refs[-1]
    start = 0
    for left, right in zip(lefts, rights):
        width = right.shape[1]
        out_ref[:, start : start + width] = tn(left[...], right[...]).astype(bf16)
        start += width
    for ref in extra:
        out_ref[:, start : start + ref.shape[1]] = ref[...]
        start += ref.shape[1]


def gradients(pairs, extra=()):
    rows, depth = pairs[0][0].shape
    size = min(512, depth)
    total = sum(right.shape[1] for _, right in pairs) + sum(x.shape[1] for x in extra)
    return pl.pallas_call(
        functools.partial(gradients_kernel, len(pairs)),
        grid=(depth // size,),
        in_specs=[pl.BlockSpec((rows, size), lambda i: (0, i)) for _ in pairs]
        + [resident(right) for _, right in pairs]
        + [row_block(size, x.shape[1]) for x in extra],
        out_specs=row_block(size, total),
        out_shape=jax.ShapeDtypeStruct((depth, total), bf16),
        compiler_params=pltpu.CompilerParams(vmem_limit_bytes=56 * MIB),
        cost_estimate=pl.CostEstimate(
            flops=2 * rows * depth * total, bytes_accessed=depth * total * 4, transcendentals=0
        ),
        name="gradients",
    )(*[left for left, _ in pairs], *[right for _, right in pairs], *extra)


def padded(width):
    return -(-width // 128) * 128


def pad_columns(weight):
    width = weight.shape[1]
    return jnp.pad(weight, ((0, 0), (0, padded(width) - width)))


def shards(inputs, cotangent, proj_in, proj_out, ffn_in, ffn_down, gains):
    rows = inputs.shape[0]
    width = proj_in.shape[2]
    depth = proj_in.shape[0]
    heads = width // HEAD_DIM
    hidden_width = ffn_down.shape[2]
    half = padded(hidden_width)
    packed = gathered(
        jnp.concatenate([proj_in[:, 0:3].reshape(depth, 3 * width), pad_columns(gains)], axis=1)
    )
    gain_rows = nt(jnp.eye(8, 5, dtype=bf16), packed[:, 3 * width : 3 * width + 5])
    gain = [gain_rows[j : j + 1] for j in range(5)]
    full0 = spread(inputs)
    w_out1 = gathered(proj_out[:, 0])
    own_pair1 = jnp.concatenate([pad_columns(ffn_in[:, j]) for j in (0, 1)], axis=1)
    own_pair2 = jnp.concatenate([pad_columns(ffn_in[:, j]) for j in (2, 3)], axis=1)
    cache_in = proj_in[:, 3:5].reshape(depth, 2, heads, HEAD_DIM).transpose(0, 2, 1, 3)
    own_cross = jnp.concatenate([cache_in.reshape(depth, 2 * width), proj_in[:, 5]], axis=1)

    normed1, own = project(full0, packed, [(gain[0], 0, 3 * width)])
    query1 = own[:, :width]
    earlier = shifted(own[:, width:], "seq", 1)
    earlier, own_pair1, own_down1 = lax.optimization_barrier(
        (earlier, own_pair1, ffn_down[:, 0])
    )
    w_pair1 = gathered(own_pair1)
    w_down1 = gathered(pad_columns(own_down1))
    w_cross = gathered(own_cross)
    w_out2 = gathered(proj_out[:, 1])
    near = jnp.concatenate([earlier, own[:, width:]], axis=0)
    key1, value1 = near[:, :width], near[:, width:]
    attended1, stats1 = near_forward(query1, key1, value1)
    full1 = chain_sum(nt(attended1, w_out1), full0, turns=1)
    branch1, saved1 = feed_forward(full1, gain[1], w_pair1, w_down1)
    full2 = chain_sum(branch1, full1)
    normed3, local_cache, normed4, query2 = project(
        full2, w_cross, [(gain[2], 0, 2 * width), (gain[3], 2 * width, width)]
    )
    local_cache, own_dout, w_out2, own_down2 = lax.optimization_barrier(
        (local_cache, cotangent, w_out2, ffn_down[:, 1])
    )
    cache_kv = gathered(local_cache)
    dfull4 = spread(own_dout)
    query2 = swapped(query2)
    query2, dfull4 = lax.optimization_barrier((query2, dfull4))
    w_down2 = gathered(pad_columns(own_down2))
    attended2, stats2 = far_forward(query2, cache_kv)
    own_attended2 = swapped(attended2)
    own_attended2, own_pair2 = lax.optimization_barrier((own_attended2, own_pair2))
    w_pair2 = gathered(own_pair2)
    full3 = chain_sum(nt(own_attended2, w_out2), full2, turns=2)
    branch2, saved2 = feed_forward(full3, gain[4], w_pair2, w_down2)

    dpart, pairs_feed2, grad_gain4 = feed_backward(dfull4, gain[4], w_pair2, w_down2, saved2)
    dfull3 = chain_sum(dpart, dfull4)
    dattended2 = swapped(nn(dfull3, w_out2).astype(bf16))
    dquery2, dcache = far_backward(query2, cache_kv, dattended2, attended2, stats2)
    dcache, branch2, pairs_feed2 = lax.optimization_barrier((dcache, branch2, pairs_feed2))
    dquery2 = swapped(dquery2)
    dcache = lax.psum_scatter(dcache, "seq", scatter_dimension=0, tiled=True)
    output = chain_sum(branch2, full3, own_only=True)
    grad_feed2 = gradients(pairs_feed2)
    dcache, output, grad_feed2 = lax.optimization_barrier((dcache, output, grad_feed2))
    grad_feed2 = scattered(grad_feed2)
    dpart, grad_gain2, grad_gain3 = project_back(
        full2,
        w_cross,
        [(gain[2], 0, 2 * width, dcache), (gain[3], 2 * width, width, dquery2)],
    )
    dpart, (grad_cross,) = together(
        dpart,
        (gradients([(normed3, dcache), (normed4, dquery2), (dfull3, own_attended2)]),),
    )
    grad_cross = scattered(grad_cross)
    dfull2 = chain_sum(dpart, dfull3, turns=3, brief=True)
    dpart, pairs_feed1, grad_gain1 = feed_backward(dfull2, gain[1], w_pair1, w_down1, saved1)
    dpart, (grad_feed1,) = together(dpart, (gradients(pairs_feed1),))
    grad_feed1 = scattered(grad_feed1)
    dpart, grad_cross = lax.optimization_barrier((dpart, grad_cross))
    dfull1 = chain_sum(dpart, dfull2, brief=True)
    dfull1, grad_feed2 = lax.optimization_barrier((dfull1, grad_feed2))
    dattended1 = nn(dfull1, w_out1).astype(bf16)
    dquery1, dkey1, dvalue1 = near_backward(query1, key1, value1, dattended1, attended1, stats1)
    dnear = jnp.concatenate([dkey1, dvalue1], axis=1)
    returned = shifted(dnear[:rows].astype(bf16), "seq", -1).astype(f32)
    grad_first = gradients([(normed1, dquery1), (dfull1, attended1)])
    dpairs = (dnear[rows:] + returned).astype(bf16)
    dself = jnp.concatenate([dquery1, dpairs], axis=1)
    dself, grad_feed1 = lax.optimization_barrier((dself, grad_feed1))
    dpart, grad_gain0 = project_back(full0, packed, [(gain[0], 0, 3 * width, dself)])
    all_gains = [grad_gain0, grad_gain1, grad_gain2, grad_gain3, grad_gain4]
    all_gains = pad_columns(jnp.concatenate(all_gains, axis=0).T.astype(bf16))
    dpart, (grad_self,) = together(
        dpart, (gradients([(normed1, dself[:, width:])], (grad_first, all_gains)),)
    )
    grad_self = scattered(grad_self)
    grad_inputs, grad_self = lax.optimization_barrier(
        (chain_sum(dpart, dfull1, own_only=True), grad_self)
    )
    total_gains = small_sum(grad_self[:, 4 * width :].astype(f32))[:, :5]
    grad_cache = grad_cross[:, : 2 * width].reshape(depth, heads, 2, HEAD_DIM)
    grad_cache = grad_cache.transpose(0, 2, 1, 3).reshape(depth, 2 * width)
    grad_in = jnp.concatenate(
        [
            grad_self[:, 2 * width : 3 * width],
            grad_self[:, : 2 * width],
            grad_cache,
            grad_cross[:, 2 * width : 3 * width],
        ],
        axis=1,
    )
    grad_out = [grad_self[:, 3 * width : 4 * width], grad_cross[:, 3 * width :]]
    grad_ffn = [
        grads[:, start : start + hidden_width]
        for grads in (grad_feed1, grad_feed2)
        for start in (0, half)
    ]
    grad_down = [grads[:, 2 * half : 2 * half + hidden_width] for grads in (grad_feed1, grad_feed2)]
    return (
        output,
        grad_inputs,
        grad_in.astype(f32).reshape(depth, 6, width),
        jnp.stack(grad_out, axis=1).astype(f32),
        jnp.stack(grad_ffn, axis=1).astype(f32),
        jnp.stack(grad_down, axis=1).astype(f32),
        total_gains,
    )


def solution(mesh):
    wide = P("seq", "tensor")
    weight = P("seq", None, "tensor")
    gain = P("seq", None)
    return jax.shard_map(
        shards,
        mesh=mesh,
        in_specs=(wide, wide, weight, weight, weight, weight, gain),
        out_specs=(wide, wide, weight, weight, weight, weight, gain),
        check_vma=False,
    )
```
